512 devices in a mesh: vec: 16 (over z, y_hi), orb: 32 (over y_lo, x, core).
Axes of the slice: x: 4, y: 8 (y_hi: 2, y_lo: 4; y = y_hi * 4 + y_lo), z: 8, core: 2. Of those that a mesh axis runs over, the one named last changes fastest.
Arguments:
- greens: bfloat16 [256, 144000], P('vec', 'orb'), may hold values from -6 to 6
- cholesky: bfloat16 [8192, 144000], P('vec', 'orb'), may hold values from -0.0625 to 0.0625
- trial_green: bfloat16 [144000], P('orb'), may hold values from -6 to 6
- gaussian: float32 [256, 8192], P('orb', 'vec'), may hold values from -6 to 6
Outputs:
- force_bias: float32 [256, 8192], P('orb', 'vec')
- potential: bfloat16 [256, 144000], P('vec', 'orb')
The draws below stay inside these ranges and needn't reach their ends.
All inputs are finite; a program needn't handle non-finite values.
Results may differ from the reference program's by a relative error of at most 0.0049.
Values may be sent and summed in bfloat16 or wider, within the bound.
A program may use at most 64 MiB of HBM per device.

```python
import jax
import jax.numpy as jnp
from jax import lax

R = 144000
NG = 8192
W = 256


def levels(rng, dims, pieces, least, largest):
    factor_of, own = 1.0, jax.random.fold_in(rng, 6)
    for dim, blocks in pieces:
        draws = jnp.exp(jax.random.uniform(jax.random.fold_in(own, dim), (blocks,), jnp.float32, least / len(pieces), largest / len(pieces)))
        factor_of = factor_of * jnp.repeat(draws, dims[dim] // blocks).reshape([-1 if axis == dim else 1 for axis in range(len(dims))])
    return factor_of


def bell_draw(key, dims, deviation, reach, split=(), held_as=jnp.bfloat16):
    entries = deviation * jax.random.normal(key, dims, jnp.float32)
    if split:
        entries = entries * levels(key, dims, split, -0.22, 0.18)
    return jnp.clip(entries, -reach, reach).astype(held_as)


def setup_inputs(seed: int = 0) -> dict:
    splits = jax.random.split(jax.random.key(seed), 5)
    return {
        "greens": bell_draw(splits[0], (W, R), 1.0, 6.0, ((0, 16), (1, 32))),
        "cholesky": bell_draw(splits[1], (NG, R), (R // 16) ** -0.5, 0.0625, ((0, 16), (1, 32))),
        "trial_green": bell_draw(splits[2], (R,), 1.0, 6.0, ((0, 32),)),
        "gaussian": bell_draw(splits[3], (W, NG), 1.0, 6.0, ((0, 32), (1, 16)), jnp.float32),
    }


sqrt_step = 0.125
cap_bound = 1.0

def reference(greens, cholesky, trial_green, gaussian):
    xbar = lax.dot_general(greens, cholesky, (((1,), (1,)), ((), ())), preferred_element_type=jnp.float32)
    mean_shift = jnp.dot(cholesky, trial_green, preferred_element_type=jnp.float32)
    force_bias = jnp.clip(sqrt_step * (xbar - mean_shift[None, :]), -cap_bound, cap_bound)
    aux_field = (gaussian - force_bias).astype(jnp.bfloat16)
    summed = jnp.dot(aux_field, cholesky, preferred_element_type=jnp.float32)
    return (force_bias, summed.astype(jnp.bfloat16))
```

```python
import functools

import jax
import jax.numpy as jnp
from jax import lax
from jax.experimental import pallas as pl
from jax.experimental.pallas import tpu as pltpu
from jax.sharding import PartitionSpec as P

MESH = pl.DeviceIdType.MESH
sqrt_step = 0.125
cap_bound = 1.0
NZ = 8
NORB = 32
RIGHT = (4, 3)
LEFT = (3, 4)
NT = (((1,), (1,)), ((), ()))
NN = (((1,), (0,)), ((), ()))


def slot(dz, p):
    return (dz % NZ) * 2 + p


def kernel(
    g_hbm, c_hbm, t_ref, n_ref, fb_ref, pot_ref,
    g_all, chol, shift, d_send, d_own, d_recv, n_all, fb_half, fb_both, aux_all, part, p_send, p_recv, y_send, y_recv,
    load_sem, a_send, a_recv, b_send, b_recv, n_sem, f_sem, c_send, c_recv, e_send, e_recv, y_sem,
):
    v, o = lax.axis_index("vec"), lax.axis_index("orb")
    z, yh = v // 2, lax.rem(v, 2)
    half = lax.rem(o, 2)
    right = (lax.rem(z + 1, NZ) * 2 + yh, o)
    left = (lax.rem(z + NZ - 1, NZ) * 2 + yh, o)
    across = (z * 2 + 1 - yh, o)
    mate = (v, o + 1 - 2 * half)

    def send(src, dst, s_sem, r_sem, device):
        return pltpu.make_async_remote_copy(
            src_ref=src, dst_ref=dst, send_sem=s_sem, recv_sem=r_sem, device_id=device, device_id_type=MESH
        )

    def block(dz, p):
        return lax.rem(z + dz % NZ, NZ) * 2 + (yh if p == 0 else 1 - yh)

    load_g = pltpu.make_async_copy(g_hbm, g_all.at[0], load_sem.at[0])
    load_c = pltpu.make_async_copy(c_hbm, chol, load_sem.at[1])
    load_g.start()
    load_c.start()

    barrier = pltpu.get_barrier_semaphore()
    for device in (right, left, across):
        pl.semaphore_signal(barrier, inc=1, device_id=device, device_id_type=MESH)

    def greet(k, _):
        pl.semaphore_signal(barrier, inc=1, device_id=(v, lax.rem(o + k, NORB)), device_id_type=MESH)
        return 0

    lax.fori_loop(1, NORB, greet, 0)
    pl.semaphore_wait(barrier, NORB + 2)

    def a_copy(p, way, step):
        sign = -1 if way == 0 else 1
        return send(
            g_all.at[slot(sign * (step - 1), p)], g_all.at[slot(sign * step, p)],
            a_send.at[p, way, step - 1], a_recv.at[p, way, step - 1], right if way == 0 else left,
        )

    load_g.wait()
    cross = send(g_all.at[0], g_all.at[1], y_sem.at[0], y_sem.at[1], across)
    a_copy(0, 0, 1).start()
    a_copy(0, 1, 1).start()
    cross.start()
    n_copy = send(
        n_ref.at[:, pl.ds(pl.multiple_of((1 - half) * 256, 256), 256)], n_all.at[half], n_sem.at[0], n_sem.at[1], mate
    )
    n_copy.start()
    n_all[half] = n_ref[:, pl.ds(pl.multiple_of(half * 256, 256), 256)]

    def products(entries, extra=None):
        rows = [g_all[slot(dz, p)] for dz, p in entries]
        if extra is not None:
            rows.append(extra)
        prod = lax.dot_general(jnp.concatenate(rows, axis=0), chol[...], NT, preferred_element_type=jnp.float32)
        if extra is not None:
            shift[...] = prod[16 * len(entries) :]
        for i, (dz, p) in enumerate(entries):
            value = prod[16 * i : 16 * i + 16] - shift[...]
            b = block(dz, p)
            for h in range(2):
                s = slot(dz, p) * 2 + h
                d_send[s] = value[:, 256 * h : 256 * h + 256]
                owner = 2 * b + h

                @pl.when(owner != o)
                def _():
                    send(
                        d_send.at[s], d_recv.at[lax.rem(o - owner + NORB, NORB) - 1], b_send, b_recv, (v, owner)
                    ).start()

                @pl.when(owner == o)
                def _():
                    d_own[...] = value[:, 256 * h : 256 * h + 256]

    def pass_on(p, step):
        for way, hops in ((0, RIGHT[p]), (1, LEFT[p])):
            if step <= hops:
                a_copy(p, way, step).wait_recv()
                if step < hops:
                    a_copy(p, way, step + 1).start()

    load_c.wait()
    products([(0, 0)], jnp.broadcast_to(t_ref[...], (16, t_ref.shape[1])))
    pass_on(0, 1)
    products([(-1, 0), (1, 0)])
    cross.wait_recv()
    a_copy(1, 0, 1).start()
    a_copy(1, 1, 1).start()
    pass_on(0, 2)
    products([(0, 1), (-2, 0), (2, 0)])
    pass_on(1, 1)
    pass_on(0, 3)
    products([(-1, 1), (1, 1)])
    products([(-3, 0), (3, 0)])
    pass_on(1, 2)
    pass_on(0, 4)
    products([(-2, 1), (2, 1), (-4, 0)])
    pass_on(1, 3)
    products([(-3, 1), (3, 1)])
    pass_on(1, 4)
    products([(4, 1)])

    n_copy.wait()
    pltpu.make_async_copy(d_recv, d_recv, b_recv).wait()

    def add(k, total):
        return total + d_recv[k]

    total = lax.fori_loop(0, NORB - 1, add, d_own[...])
    capped = jnp.clip(sqrt_step * total, -cap_bound, cap_bound)
    noise = jnp.concatenate([n_all[0], n_all[1]], axis=0)
    aux_all[o] = (noise - capped).astype(jnp.bfloat16)

    def c_copy(k, _):
        send(aux_all.at[o], aux_all.at[o], c_send, c_recv, (v, lax.rem(o + k, NORB))).start()
        return 0

    lax.fori_loop(1, NORB, c_copy, 0)
    fb_half[0] = capped[:8]
    fb_half[1] = capped[8:]
    f_copy = send(fb_half.at[1 - half], fb_both.at[half], f_sem.at[0], f_sem.at[1], mate)
    f_copy.start()
    fb_both[half] = fb_half[half]
    pltpu.make_async_copy(aux_all.at[pl.ds(0, NORB - 1)], aux_all.at[pl.ds(0, NORB - 1)], c_recv).wait()

    def potential(dest, entries):
        rows = []
        for dz, p in entries:
            b = block(dz, p)
            rows.append(jnp.concatenate([aux_all[2 * b], aux_all[2 * b + 1]], axis=1))
        lhs = jnp.concatenate(rows, axis=0)
        width = part.shape[2]
        for j in range(0, width, 512):
            m = min(512, width - j)
            part[dest, : lhs.shape[0], j : j + m] = lax.dot_general(
                lhs, chol[:, j : j + m], NN, preferred_element_type=jnp.float32
            )

    def e_copy(p, way, step):
        i = (p * 2 + way) * 4 + step - 1
        return send(
            p_send.at[i], p_recv.at[i], e_send.at[i], e_recv.at[i], right if way == 0 else left
        )

    def hop(p, step):
        i = 0
        ways = [(w, n) for w, n in ((0, RIGHT[p]), (1, LEFT[p])) if step <= n]
        sign = {0: 1, 1: -1}
        potential(p, [(sign[w] * (n - step + 1), p) for w, n in ways])
        for i, (w, _) in enumerate(ways):
            value = part[p, 16 * i : 16 * i + 16, :]
            if step > 1:
                e_copy(p, w, step - 1).wait_recv()
                value = value + p_recv[(p * 2 + w) * 4 + step - 2].astype(jnp.float32)
            p_send[(p * 2 + w) * 4 + step - 1] = value.astype(jnp.bfloat16)
            e_copy(p, w, step).start()

    def last(p):
        value = part[2, 16 * p : 16 * p + 16, :]
        for w, n in ((0, RIGHT[p]), (1, LEFT[p])):
            e_copy(p, w, n).wait_recv()
            value = value + p_recv[(p * 2 + w) * 4 + n - 1].astype(jnp.float32)
        return value

    for step in (1, 2, 3, 4):
        hop(1, step)
        hop(0, step)
    potential(2, [(0, 0), (0, 1)])
    y_send[...] = last(1).astype(jnp.bfloat16)
    back = send(y_send, y_recv, y_sem.at[2], y_sem.at[3], across)
    back.start()
    mine = last(0)
    f_copy.wait()
    fb_ref[:, :256] = fb_both[0]
    fb_ref[:, 256:] = fb_both[1]
    back.wait_recv()
    pot_ref[...] = (mine + y_recv[...].astype(jnp.float32)).astype(jnp.bfloat16)

    cross.wait_send()
    back.wait_send()
    for p in range(2):
        for way, hops in ((0, RIGHT[p]), (1, LEFT[p])):
            for step in range(1, hops + 1):
                a_copy(p, way, step).wait_send()
                e_copy(p, way, step).wait_send()
    pltpu.make_async_copy(d_recv, d_recv, b_send).wait()
    pltpu.make_async_copy(aux_all.at[pl.ds(0, NORB - 1)], aux_all.at[pl.ds(0, NORB - 1)], c_send).wait()


def local(greens, cholesky, trial_green, gaussian):
    walkers, pairs = greens.shape
    vectors = cholesky.shape[0]
    bf, f4, vm = jnp.bfloat16, jnp.float32, pltpu.VMEM
    dma = pltpu.SemaphoreType.DMA
    return pl.pallas_call(
        kernel,
        out_shape=(
            jax.ShapeDtypeStruct(gaussian.shape, f4),
            jax.ShapeDtypeStruct(greens.shape, bf),
        ),
        in_specs=[pl.BlockSpec(memory_space=pl.ANY)] * 2 + [pl.BlockSpec(memory_space=vm)] * 2,
        out_specs=(pl.BlockSpec(memory_space=vm),) * 2,
        scratch_shapes=[
            vm((2 * NZ, walkers, pairs), bf),
            vm((vectors, pairs), bf),
            vm((walkers, vectors), f4),
            vm((4 * NZ, 16, 256), f4),
            vm((16, 256), f4),
            vm((NORB - 1, 16, 256), f4),
            vm((2, 8, 256), f4),
            vm((2, 8, 256), f4),
            vm((2, 8, 256), f4),
            vm((NORB, 16, 256), bf),
            vm((3, 2 * walkers, pairs), f4),
            vm((16, walkers, pairs), bf),
            vm((16, walkers, pairs), bf),
            vm((walkers, pairs), bf),
            vm((walkers, pairs), bf),
            dma((2,)),
            dma((2, 2, 4)),
            dma((2, 2, 4)),
            dma(()),
            dma(()),
            dma((2,)),
            dma((2,)),
            dma(()),
            dma(()),
            dma((16,)),
            dma((16,)),
            dma((4,)),
        ],
        compiler_params=pltpu.CompilerParams(
            collective_id=0, has_side_effects=True, vmem_limit_bytes=40 << 20
        ),
        cost_estimate=pl.CostEstimate(flops=2400000000, bytes_accessed=5200000, transcendentals=0),
    )(greens, cholesky, trial_green.reshape(1, pairs), gaussian)


def solution(mesh):
    in_specs = (P("vec", "orb"), P("vec", "orb"), P("orb"), P("orb", "vec"))
    out_specs = (P("orb", "vec"), P("vec", "orb"))
    return jax.shard_map(local, mesh=mesh, in_specs=in_specs, out_specs=out_specs, check_vma=False)
```

```python
import jax
import jax.numpy as jnp
from jax import lax
from jax.experimental import pallas as pl
from jax.experimental.pallas import tpu as pltpu
from jax.sharding import PartitionSpec as P

MESH = pl.DeviceIdType.MESH
sqrt_step = 0.125
cap_bound = 1.0
NZ = 8
NORB = 32
PAIRS = 4500
WIDE = 1536
NC = -(-PAIRS // WIDE)
WIDTHS = [min(WIDE, PAIRS - WIDE * c) for c in range(NC)]
HOPS = ((4, 3), (3, 4))
NT = (((1,), (1,)), ((), ()))
NN = (((1,), (0,)), ((), ()))


def slot(dz, p):
    return (dz % NZ) * 2 + p


def kernel(
    g_in, c_hbm, t_ref, n_ref, fb_ref, pot_ref,
    g_all, chol, shift, d_send, d_own, d_recv, n_all, fb_half, fb_both, aux_all, p_send, p_recv, y_send, y_recv,
    load_sem, a_send, a_recv, b_send, b_recv, n_sem, f_sem, c_send, c_recv, e_send, e_recv, y_sem, y_back,
):
    v, o = lax.axis_index("vec"), lax.axis_index("orb")
    z, yh = v // 2, lax.rem(v, 2)
    half = lax.rem(o, 2)
    kind = jnp.where(lax.rem(o // 2, 2) == yh, 0, 1)
    sides = ((lax.rem(z + 1, NZ) * 2 + yh, o), (lax.rem(z + NZ - 1, NZ) * 2 + yh, o))
    across = (z * 2 + 1 - yh, o)
    mate = (v, o + 1 - 2 * half)

    def send(src, dst, s_sem, r_sem, device):
        return pltpu.make_async_remote_copy(
            src_ref=src, dst_ref=dst, send_sem=s_sem, recv_sem=r_sem, device_id=device, device_id_type=MESH
        )

    def block(dz, p):
        return lax.rem(z + dz % NZ, NZ) * 2 + (yh if p == 0 else 1 - yh)

    load_c = pltpu.make_async_copy(c_hbm, chol, load_sem)
    barrier = pltpu.get_barrier_semaphore()
    for device in (*sides, across):
        pl.semaphore_signal(barrier, inc=1, device_id=device, device_id_type=MESH)

    def greet(k, _):
        pl.semaphore_signal(barrier, inc=1, device_id=(v, lax.rem(o + k, NORB)), device_id_type=MESH)
        return 0

    lax.fori_loop(1, NORB, greet, 0)
    load_c.start()

    if WIDTHS[-1] != WIDE:
        g_all[0, NC - 1] = jnp.zeros((16, WIDE), jnp.bfloat16)
    for c in range(NC):
        g_all[0, c, :, : WIDTHS[c]] = g_in[:, WIDE * c : WIDE * c + WIDTHS[c]]
    pl.semaphore_wait(barrier, NORB + 2)

    def a_copy(p, way, step, c):
        sign = 1 if way else -1
        i = ((p * 2 + way) * 4 + step - 1) * NC + c
        return send(
            g_all.at[slot(sign * (step - 1), p), c], g_all.at[slot(sign * step, p), c], a_send.at[i], a_recv.at[i], sides[way]
        )

    def cross(c):
        return send(g_all.at[0, c], g_all.at[1, c], y_sem.at[0, c], y_sem.at[1, c], across)

    for c in range(NC):
        a_copy(0, 0, 1, c).start()
        a_copy(0, 1, 1, c).start()
    for c in range(NC):
        cross(c).start()
    n_copy = send(
        n_ref.at[:, pl.ds(pl.multiple_of((1 - half) * 256, 256), 256)], n_all.at[half], n_sem.at[0], n_sem.at[1], mate
    )
    n_copy.start()
    n_all[half] = n_ref[:, pl.ds(pl.multiple_of(half * 256, 256), 256)]

    def product(lhs, c):
        return lax.dot_general(
            lhs, chol[WIDE * c : WIDE * c + WIDTHS[c], :], NN, preferred_element_type=jnp.float32
        )

    def rows(entries, c):
        return jnp.concatenate([g_all[slot(dz, p), c, :, : WIDTHS[c]] for dz, p in entries], axis=0)

    def to_owners(entries, prod):
        for i, (dz, p) in enumerate(entries):
            value = prod[16 * i : 16 * i + 16] - shift[...]
            b = block(dz, p)
            for h in range(2):
                s = slot(dz, p) * 2 + h
                d_send[s] = value[:, 256 * h : 256 * h + 256]
                owner = 2 * b + h

                @pl.when(owner != o)
                def _():
                    send(
                        d_send.at[s], d_recv.at[lax.rem(o - owner + NORB, NORB) - 1], b_send, b_recv, (v, owner)
                    ).start()

                @pl.when(owner == o)
                def _():
                    d_own[...] = value[:, 256 * h : 256 * h + 256]

    def gather(p, step, more=()):
        ways = [w for w in range(2) if step <= HOPS[p][w]]
        entries = [((step if w else -step), p) for w in ways] + list(more)
        prod = None
        for c in range(NC):
            for w in ways:
                a_copy(p, w, step, c).wait_recv()
                if step < HOPS[p][w]:
                    a_copy(p, w, step + 1, c).start()
            term = product(rows(entries, c), c)
            prod = term if prod is None else prod + term
        to_owners(entries, prod)

    def fields():
        n_copy.wait_recv()
        pltpu.make_async_copy(d_recv, d_recv, b_recv).wait()
        total = lax.fori_loop(0, NORB - 1, lambda k, t: t + d_recv[k], d_own[...])
        capped = jnp.clip(sqrt_step * total, -cap_bound, cap_bound)
        noise = jnp.concatenate([n_all[0], n_all[1]], axis=0)
        aux_all[o] = (noise - capped).astype(jnp.bfloat16)

        def c_copy(k, _):
            send(aux_all.at[o], aux_all.at[o], c_send, c_recv.at[kind], (v, lax.rem(o + k, NORB))).start()
            return 0

        lax.fori_loop(1, NORB, c_copy, 0)
        fb_half[0] = capped[:8]
        fb_half[1] = capped[8:]
        send(fb_half.at[1 - half], fb_both.at[half], f_sem.at[0], f_sem.at[1], mate).start()
        fb_both[half] = fb_half[half]

    def fields_there(p):
        for n, is_own in ((15, kind == p), (16, kind != p)):

            @pl.when(is_own)
            def _():
                pltpu.make_async_copy(aux_all.at[pl.ds(0, n)], aux_all.at[pl.ds(0, n)], c_recv.at[p]).wait()

    load_c.wait()
    first = None
    for c in range(NC):
        trial = jnp.broadcast_to(t_ref[WIDE * c : WIDE * c + WIDTHS[c]][None, :], (16, WIDTHS[c]))
        term = product(jnp.concatenate([rows([(0, 0)], c), trial], axis=0), c)
        first = term if first is None else first + term
    shift[...] = first[16:]
    to_owners([(0, 0)], first[:16])
    gather(0, 1)
    gather(0, 2)
    for c in range(NC):
        cross(c).wait_recv()
        a_copy(1, 1, 1, c).start()
    gather(0, 3)
    for c in range(NC):
        a_copy(1, 0, 1, c).start()
    gather(0, 4, [(0, 1)])
    gather(1, 1)

    @pl.when(kind == 0)
    def _():
        fields()

    gather(1, 2)
    gather(1, 3)
    gather(1, 4)

    def fields_of(entries):
        parts = []
        for dz, p in entries:
            b = block(dz, p)
            parts.append(jnp.concatenate([aux_all[2 * b], aux_all[2 * b + 1]], axis=1))
        return jnp.concatenate(parts, axis=0)

    def potential(lhs, c):
        return lax.dot_general(lhs, chol[WIDE * c : WIDE * c + WIDTHS[c], :], NT, preferred_element_type=jnp.float32)

    def e_index(p, way, step):
        return (p * 2 + way) * 4 + step - 1

    def e_copy(p, way, step, c):
        i = e_index(p, way, step)
        return send(p_send.at[i, c], p_recv.at[i, c], e_send.at[i * NC + c], e_recv.at[i * NC + c], sides[way])

    def arrived(p, way, step, c):
        e_copy(p, way, step, c).wait_recv()
        return p_recv[e_index(p, way, step), c, :, : WIDTHS[c]].astype(jnp.float32)

    def hop(p, step):
        ways = [w for w in range(2) if step <= HOPS[p][w]]
        lhs = fields_of([((1 - 2 * w) * (HOPS[p][w] - step + 1), p) for w in ways])
        for c in range(NC):
            value = potential(lhs, c)
            for i, w in enumerate(ways):
                own = value[16 * i : 16 * i + 16]
                if step > 1:
                    own = own + arrived(p, w, step - 1, c)
                p_send[e_index(p, w, step), c, :, : WIDTHS[c]] = own.astype(jnp.bfloat16)
                e_copy(p, w, step, c).start()

    def back(c):
        return send(y_send.at[c], y_recv.at[c], y_back.at[0, c], y_back.at[1, c], across)

    fields_there(0)
    hop(0, 1)

    @pl.when(kind == 1)
    def _():
        fields()

    hop(0, 2)
    fields_there(1)
    hop(1, 1)
    hop(1, 2)
    hop(1, 3)
    hop(1, 4)
    hop(0, 3)
    lhs = fields_of([(0, 1)])
    for c in range(NC):
        value = potential(lhs, c)
        for w in range(2):
            value = value + arrived(1, w, HOPS[1][w], c)
        y_send[c, :, : WIDTHS[c]] = value.astype(jnp.bfloat16)
        back(c).start()
    hop(0, 4)
    send(fb_half.at[1 - half], fb_both.at[half], f_sem.at[0], f_sem.at[1], mate).wait()
    fb_ref[:, :256] = fb_both[0]
    fb_ref[:, 256:] = fb_both[1]
    lhs = fields_of([(0, 0)])
    for c in range(NC):
        value = potential(lhs, c)
        for w in range(2):
            value = value + arrived(0, w, HOPS[0][w], c)
        back(c).wait_recv()
        value = value + y_recv[c, :, : WIDTHS[c]].astype(jnp.float32)
        pot_ref[:, WIDE * c : WIDE * c + WIDTHS[c]] = value.astype(jnp.bfloat16)

    n_copy.wait_send()
    for c in range(NC):
        cross(c).wait_send()
        back(c).wait_send()
        for p in range(2):
            for way in range(2):
                for step in range(1, HOPS[p][way] + 1):
                    a_copy(p, way, step, c).wait_send()
                    e_copy(p, way, step, c).wait_send()
    pltpu.make_async_copy(d_recv, d_recv, b_send).wait()
    pltpu.make_async_copy(aux_all.at[pl.ds(0, NORB - 1)], aux_all.at[pl.ds(0, NORB - 1)], c_send).wait()


def local(greens, cholesky, trial_green, gaussian):
    walkers, pairs = greens.shape
    vectors = cholesky.shape[0]
    bf, f4, vm = jnp.bfloat16, jnp.float32, pltpu.VMEM
    dma = pltpu.SemaphoreType.DMA
    return pl.pallas_call(
        kernel,
        out_shape=(
            jax.ShapeDtypeStruct(gaussian.shape, f4),
            jax.ShapeDtypeStruct(greens.shape, bf),
        ),
        in_specs=[pl.BlockSpec(memory_space=m) for m in (vm, pl.ANY, vm, vm)],
        out_specs=(pl.BlockSpec(memory_space=vm),) * 2,
        scratch_shapes=[
            vm((2 * NZ, NC, walkers, WIDE), bf),
            vm((pairs, vectors), bf),
            vm((walkers, vectors), f4),
            vm((4 * NZ, 16, 256), f4),
            vm((16, 256), f4),
            vm((NORB - 1, 16, 256), f4),
            vm((2, 8, 256), f4),
            vm((2, 8, 256), f4),
            vm((2, 8, 256), f4),
            vm((NORB, 16, 256), bf),
            vm((16, NC, walkers, WIDE), bf),
            vm((16, NC, walkers, WIDE), bf),
            vm((NC, walkers, WIDE), bf),
            vm((NC, walkers, WIDE), bf),
            dma(()),
            dma((16 * NC,)),
            dma((16 * NC,)),
            dma(()),
            dma(()),
            dma((2,)),
            dma((2,)),
            dma(()),
            dma((2,)),
            dma((16 * NC,)),
            dma((16 * NC,)),
            dma((2, NC)),
            dma((2, NC)),
        ],
        compiler_params=pltpu.CompilerParams(
            collective_id=0, has_side_effects=True, vmem_limit_bytes=50 << 20
        ),
        cost_estimate=pl.CostEstimate(flops=2400000000, bytes_accessed=5200000, transcendentals=0),
    )(greens, cholesky.T, trial_green, gaussian)


def solution(mesh):
    in_specs = (P("vec", "orb"), P("vec", "orb"), P("orb"), P("orb", "vec"))
    out_specs = (P("orb", "vec"), P("vec", "orb"))
    return jax.shard_map(local, mesh=mesh, in_specs=in_specs, out_specs=out_specs, check_vma=False)
```

```python
import jax
import jax.numpy as jnp
from jax import lax
from jax.experimental import pallas as pl
from jax.experimental.pallas import tpu as pltpu
from jax.sharding import PartitionSpec as P

MESH = pl.DeviceIdType.MESH
sqrt_step = 0.125
cap_bound = 1.0
NZ = 8
NORB = 32
PAIRS = 4500
WIDE = 1536
NC = -(-PAIRS // WIDE)
WIDTHS = [min(WIDE, PAIRS - WIDE * c) for c in range(NC)]
HOPS = ((4, 3), (3, 4))
NT = (((1,), (1,)), ((), ()))
NN = (((1,), (0,)), ((), ()))


def slot(dz, p):
    return (dz % NZ) * 2 + p


def kernel(
    g_in, c_hbm, t_ref, n_ref, fb_ref, pot_ref,
    g_all, chol, shift, keep, m_send, m_recv, d_send, w_send, d_own, d_recv, w_recv, n_all, fb_half, fb_both, aux_all, p_send, p_recv, y_send, y_recv,
    load_sem, a_send, a_recv, m_out, m_in, b_send, b_recv, n_sem, f_sem, c_send, c_recv, t_send, t_recv, e_send, e_recv, y_sem, y_back,
):
    v, o = lax.axis_index("vec"), lax.axis_index("orb")
    z, yh = v // 2, lax.rem(v, 2)
    half = lax.rem(o, 2)
    kind = jnp.where(lax.rem(o // 2, 2) == yh, 0, 1)
    sides = ((lax.rem(z + 1, NZ) * 2 + yh, o), (lax.rem(z + NZ - 1, NZ) * 2 + yh, o))
    across = (z * 2 + 1 - yh, o)
    mate = (v, o + 1 - 2 * half)

    def send(src, dst, s_sem, r_sem, device):
        return pltpu.make_async_remote_copy(
            src_ref=src, dst_ref=dst, send_sem=s_sem, recv_sem=r_sem, device_id=device, device_id_type=MESH
        )

    def block(dz, p):
        return lax.rem(z + dz % NZ, NZ) * 2 + (yh if p == 0 else 1 - yh)

    load_c = pltpu.make_async_copy(c_hbm, chol, load_sem)
    barrier = pltpu.get_barrier_semaphore()
    for device in (*sides, across, mate):
        pl.semaphore_signal(barrier, inc=1, device_id=device, device_id_type=MESH)

    def greet(k, _):
        pl.semaphore_signal(barrier, inc=1, device_id=(v, lax.rem(o + 2 * k, NORB)), device_id_type=MESH)
        return 0

    lax.fori_loop(1, NORB // 2, greet, 0)
    load_c.start()

    if WIDTHS[-1] != WIDE:
        g_all[0, NC - 1] = jnp.zeros((16, WIDE), jnp.bfloat16)
    for c in range(NC):
        g_all[0, c, :, : WIDTHS[c]] = g_in[:, WIDE * c : WIDE * c + WIDTHS[c]]
    pl.semaphore_wait(barrier, NORB // 2 + 3)

    def a_copy(p, way, step, c):
        sign = 1 if way else -1
        i = ((p * 2 + way) * 4 + step - 1) * NC + c
        return send(
            g_all.at[slot(sign * (step - 1), p), c], g_all.at[slot(sign * step, p), c], a_send.at[i], a_recv.at[i], sides[way]
        )

    def cross(c):
        return send(g_all.at[0, c], g_all.at[1, c], y_sem.at[0, c], y_sem.at[1, c], across)

    for c in range(NC):
        a_copy(0, 0, 1, c).start()
        a_copy(0, 1, 1, c).start()
        cross(c).start()
    n_copy = send(
        n_ref.at[:, pl.ds(pl.multiple_of((1 - half) * 256, 256), 256)], n_all.at[half], n_sem.at[0], n_sem.at[1], mate
    )
    n_copy.start()
    n_all[half] = n_ref[:, pl.ds(pl.multiple_of(half * 256, 256), 256)]

    def product(lhs, c):
        return lax.dot_general(
            lhs, chol[WIDE * c : WIDE * c + WIDTHS[c], :], NN, preferred_element_type=jnp.float32
        )

    def rows(entries, c):
        return jnp.concatenate([g_all[slot(dz, p), c, :, : WIDTHS[c]] for dz, p in entries], axis=0)

    def pair_copy(dz, p):
        i = slot(dz, p)
        return send(m_send.at[i], m_recv.at[i], m_out.at[i], m_in.at[i], mate)

    def to_mate(entries, prod):
        for i, (dz, p) in enumerate(entries):
            value = prod[16 * i : 16 * i + 16] - shift[...]
            low, high = value[:, :256], value[:, 256:]
            keep[slot(dz, p)] = jnp.where(half == 0, low, high)
            m_send[slot(dz, p)] = jnp.where(half == 0, high, low)
            pair_copy(dz, p).start()

    def to_owners(entries):
        for dz, p in entries:
            pair_copy(dz, p).wait_recv()
            total = keep[slot(dz, p)] + m_recv[slot(dz, p)]
            b = block(dz, p)
            out, into = ((d_send, d_recv), (w_send, w_recv))[p]
            out[dz % NZ] = total.astype(out.dtype)
            place = lax.rem(o // 2 - b + 16, 16)

            @pl.when(place != 0)
            def _():
                send(out.at[dz % NZ], into.at[place - 1], b_send.at[p], b_recv.at[p], (v, 2 * b + half)).start()

            @pl.when(place == 0)
            def _():
                d_own[...] = total

    def gather(p, step, more=(), before=(), first=False):
        ways = [w for w in range(2) if step <= HOPS[p][w]]
        entries = [((step if w else -step), p) for w in ways] + list(more)
        prod = None
        for c in range(NC):
            for w in ways:
                a_copy(p, w, step, c).wait_recv()
                if step < HOPS[p][w]:
                    a_copy(p, w, step + 1, c).start()
            if c == 0:
                to_owners(before)
            lhs = rows(entries, c)
            if first:
                trial = t_ref[WIDE * c : WIDE * c + WIDTHS[c]][None, :]
                lhs = jnp.concatenate([lhs, jnp.broadcast_to(trial, (16, WIDTHS[c]))], axis=0)
                if c == 0:
                    load_c.wait()
            term = product(lhs, c)
            prod = term if prod is None else prod + term
        if first:
            shift[...] = prod[16 * len(entries) :]
        to_mate(entries, prod)
        return entries

    def fields(p):
        n_copy.wait_recv()
        into = (d_recv, w_recv)[p]
        pltpu.make_async_copy(into, into, b_recv.at[p]).wait()
        total = d_own[...]
        for k in range(15):
            total = total + into[k].astype(jnp.float32)
        capped = jnp.clip(sqrt_step * total, -cap_bound, cap_bound)
        noise = jnp.concatenate([n_all[0], n_all[1]], axis=0)
        mine = aux_all.at[half, lax.rem(o // 2, 2), o // 4]
        mine[...] = (noise - capped).astype(jnp.bfloat16)

        def c_copy(k, _):
            send(mine, mine, c_send, c_recv.at[p], (v, lax.rem(o + 2 * k, NORB))).start()
            return 0

        lax.fori_loop(1, NORB // 2, c_copy, 0)
        fb_half[0] = capped[:8]
        fb_half[1] = capped[8:]
        send(fb_half.at[1 - half], fb_both.at[half], f_sem.at[0], f_sem.at[1], mate).start()
        fb_both[half] = fb_half[half]

    def turn(p):
        half_fields = aux_all.at[half, yh if p == 0 else 1 - yh]
        return send(half_fields, half_fields, t_send.at[p], t_recv.at[p], mate)

    def to_turn(p):
        for n, is_own in ((7, kind == p), (8, kind != p)):

            @pl.when(is_own)
            def _():
                pltpu.make_async_copy(aux_all.at[0, 0, pl.ds(0, n)], aux_all.at[0, 0, pl.ds(0, n)], c_recv.at[p]).wait()

        turn(p).start()

    done = gather(0, 1, [(0, 0)], first=True)
    done = gather(0, 2, before=done)
    for c in range(NC):
        cross(c).wait_recv()
        a_copy(1, 1, 1, c).start()
    done = gather(0, 3, before=done)
    for c in range(NC):
        a_copy(1, 0, 1, c).start()
    done = gather(0, 4, [(0, 1)], before=done)
    done = gather(1, 1, before=done)

    @pl.when(kind == 0)
    def _():
        fields(0)


    done = gather(1, 2, before=done)

    done = gather(1, 3, before=done)
    to_turn(0)
    done = gather(1, 4, before=done)

    def fields_of(entries):
        parts = []
        for dz, p in entries:
            q, at = (yh if p == 0 else 1 - yh), lax.rem(z + dz % NZ, NZ)
            parts.append(jnp.concatenate([aux_all[0, q, at], aux_all[1, q, at]], axis=1))
        return jnp.concatenate(parts, axis=0)

    def potential(lhs, c):
        return lax.dot_general(lhs, chol[WIDE * c : WIDE * c + WIDTHS[c], :], NT, preferred_element_type=jnp.float32)

    def e_index(p, way, step):
        return (p * 2 + way) * 4 + step - 1

    def e_copy(p, way, step, c):
        i = e_index(p, way, step)
        return send(p_send.at[i, c], p_recv.at[i, c], e_send.at[i * NC + c], e_recv.at[i * NC + c], sides[way])

    def arrived(p, way, step, c):
        e_copy(p, way, step, c).wait_recv()
        return p_recv[e_index(p, way, step), c, :, : WIDTHS[c]].astype(jnp.float32)

    def hop(p, step):
        ways = [w for w in range(2) if step <= HOPS[p][w]]
        lhs = fields_of([((1 - 2 * w) * (HOPS[p][w] - step + 1), p) for w in ways])
        for c in range(NC):
            value = potential(lhs, c)
            for i, w in enumerate(ways):
                own = value[16 * i : 16 * i + 16]
                if step > 1:
                    own = own + arrived(p, w, step - 1, c)
                p_send[e_index(p, w, step), c, :, : WIDTHS[c]] = own.astype(jnp.bfloat16)
                e_copy(p, w, step, c).start()

    def back(c):
        return send(y_send.at[c], y_recv.at[c], y_back.at[0, c], y_back.at[1, c], across)

    turn(0).wait_recv()
    hop(0, 1)
    to_owners(done)

    @pl.when(kind == 1)
    def _():
        fields(1)

    hop(0, 2)
    to_turn(1)
    hop(0, 3)
    turn(1).wait_recv()
    hop(1, 1)
    hop(1, 2)
    hop(1, 3)
    hop(1, 4)
    lhs = fields_of([(0, 1)])
    for c in range(NC):
        value = potential(lhs, c)
        for w in range(2):
            value = value + arrived(1, w, HOPS[1][w], c)
        y_send[c, :, : WIDTHS[c]] = value.astype(jnp.bfloat16)
        back(c).start()
    hop(0, 4)
    send(fb_half.at[1 - half], fb_both.at[half], f_sem.at[0], f_sem.at[1], mate).wait()
    fb_ref[:, :256] = fb_both[0]
    fb_ref[:, 256:] = fb_both[1]
    lhs = fields_of([(0, 0)])
    for c in range(NC):
        value = potential(lhs, c)
        for w in range(2):
            value = value + arrived(0, w, HOPS[0][w], c)
        back(c).wait_recv()
        value = value + y_recv[c, :, : WIDTHS[c]].astype(jnp.float32)
        pot_ref[:, WIDE * c : WIDE * c + WIDTHS[c]] = value.astype(jnp.bfloat16)

    n_copy.wait_send()
    for c in range(NC):
        cross(c).wait_send()
        back(c).wait_send()
        for p in range(2):
            for way in range(2):
                for step in range(1, HOPS[p][way] + 1):
                    a_copy(p, way, step, c).wait_send()
                    e_copy(p, way, step, c).wait_send()
    for p, buffer in enumerate((d_send, w_send)):
        for n, is_own in ((7, kind == p), (8, kind != p)):

            @pl.when(is_own)
            def _():
                pltpu.make_async_copy(buffer.at[pl.ds(0, n)], buffer.at[pl.ds(0, n)], b_send.at[p]).wait()

        for dz in range(NZ):
            pair_copy(dz, p).wait_send()
    pltpu.make_async_copy(w_recv, w_recv, c_send).wait()
    turn(0).wait_send()
    turn(1).wait_send()


def local(greens, cholesky, trial_green, gaussian):
    walkers, pairs = greens.shape
    vectors = cholesky.shape[0]
    bf, f4, vm = jnp.bfloat16, jnp.float32, pltpu.VMEM
    dma = pltpu.SemaphoreType.DMA
    return pl.pallas_call(
        kernel,
        out_shape=(
            jax.ShapeDtypeStruct(gaussian.shape, f4),
            jax.ShapeDtypeStruct(greens.shape, bf),
        ),
        in_specs=[pl.BlockSpec(memory_space=m) for m in (vm, pl.ANY, vm, vm)],
        out_specs=(pl.BlockSpec(memory_space=vm),) * 2,
        scratch_shapes=[
            vm((2 * NZ, NC, walkers, WIDE), bf),
            vm((pairs, vectors), bf),
            vm((walkers, vectors), f4),
            vm((2 * NZ, 16, 256), f4),
            vm((2 * NZ, 16, 256), f4),
            vm((2 * NZ, 16, 256), f4),
            vm((NZ, 16, 256), f4),
            vm((NZ, 16, 256), bf),
            vm((16, 256), f4),
            vm((NORB // 2 - 1, 16, 256), f4),
            vm((NORB // 2 - 1, 16, 256), bf),
            vm((2, 8, 256), f4),
            vm((2, 8, 256), f4),
            vm((2, 8, 256), f4),
            vm((2, 2, NZ, 16, 256), bf),
            vm((16, NC, walkers, WIDE), bf),
            vm((16, NC, walkers, WIDE), bf),
            vm((NC, walkers, WIDE), bf),
            vm((NC, walkers, WIDE), bf),
            dma(()),
            dma((16 * NC,)),
            dma((16 * NC,)),
            dma((2 * NZ,)),
            dma((2 * NZ,)),
            dma((2,)),
            dma((2,)),
            dma((2,)),
            dma((2,)),
            dma(()),
            dma((2,)),
            dma((2,)),
            dma((2,)),
            dma((16 * NC,)),
            dma((16 * NC,)),
            dma((2, NC)),
            dma((2, NC)),
        ],
        compiler_params=pltpu.CompilerParams(
            collective_id=0, has_side_effects=True, vmem_limit_bytes=50 << 20
        ),
        cost_estimate=pl.CostEstimate(flops=2400000000, bytes_accessed=5200000, transcendentals=0),
    )(greens, cholesky.T, trial_green, gaussian)


def solution(mesh):
    in_specs = (P("vec", "orb"), P("vec", "orb"), P("orb"), P("orb", "vec"))
    out_specs = (P("orb", "vec"), P("vec", "orb"))
    return jax.shard_map(local, mesh=mesh, in_specs=in_specs, out_specs=out_specs, check_vma=False)
```
